32 devices in a mesh: ap: 8 (over z, x), ut: 4 (over y, core).
Axes of the slice: x: 2, y: 2, z: 4, core: 2. Of those that a mesh axis runs over, the one named last changes fastest.
Arguments:
- channel: bfloat16 [2, 2, 32, 64, 1024], P(None, None, 'ap', None, 'ut'), may hold values from -0.00390625 to 0.00390625
- start_precoder: bfloat16 [2, 2, 32, 64, 1024], P(None, None, 'ap', None, 'ut'), may hold values from -6 to 6
- cluster: int32 [32, 4], P('ap', 'ut'), may hold values 0 or 1
- noise: float32 [2, 1024], P(None, 'ut'), may hold values from 0.2 to 2
- penalty: float32 [32], P('ap'), may hold values from 2.3841858e-08 to 4.7683716e-07
- power: float32 [32], P('ap'), may hold values from 0.5 to 2
Outputs:
- precoder: bfloat16 [2, 2, 32, 64, 1024], P(None, None, 'ap', None, 'ut')
- user_weight: float32 [2, 1024], P(None, 'ut')
The draws below stay inside these ranges and needn't reach their ends.
All inputs are finite; a program needn't handle non-finite values. No bound on the sum of `cluster` on one device may be relied on, other than what follows from the above.
Results may differ from the reference program's by a relative error of at most 0.003.
Values may be sent and summed in bfloat16 or wider, within the bound.
A program may use at most 64 MiB of HBM per device.

```python
import math
import jax
import jax.numpy as jnp
from jax import lax

M = 64
S = 2
ITERS = 1
U_ALL = 1024
AP_ALL = 32
TILES = 4


def with_ends(values, rng, least, largest):
    place = [jax.random.randint(jax.random.fold_in(rng, axis), (), 0, length) for axis, length in enumerate(values.shape)]
    longest = values.shape.index(max(values.shape))
    next_to = place[:longest] + [(place[longest] + 1) % values.shape[longest]] + place[longest + 1:]
    return values.at[tuple(place)].set(least).at[tuple(next_to)].set(largest)


def block_scale(own_key, dims, shards, least, top_value):
    def one(dim, shards_of):
        draws = jax.random.uniform(jax.random.fold_in(jax.random.fold_in(own_key, 6), dim), (shards_of,), jnp.float32, least / len(shards), top_value / len(shards))
        return jnp.repeat(jnp.exp(draws), dims[dim] // shards_of).reshape((-1,) + (1,) * (len(dims) - dim - 1))

    factor_of = one(*shards[0])
    for cut in shards[1:]:
        factor_of = factor_of * one(*cut)
    return factor_of


def centred(own_key, extent, spread, most, pieces=(), kind=jnp.bfloat16):
    level = block_scale(own_key, extent, pieces, -0.22, 0.18) if pieces else 1.0
    entries = jax.random.normal(own_key, extent, jnp.float32) * spread * level
    return jnp.minimum(jnp.maximum(entries, -most), most).astype(kind)


def setup_inputs(seed: int = 0) -> dict:
    seeds = jax.random.split(jax.random.key(seed), 7)
    channel = centred(seeds[0], (S, 2, AP_ALL, M, U_ALL), ((M * AP_ALL * U_ALL) ** -0.5), 0.00390625, ((2, 8), (4, 4)))
    start_precoder = centred(seeds[1], (S, 2, AP_ALL, M, U_ALL), 1.0, 6.0, ((2, 8), (4, 4)))
    cluster = with_ends((jax.random.randint(seeds[2], (AP_ALL, TILES), 0, 2) < 1).astype(jnp.int32), jax.random.fold_in(seeds[2], 1), 0, 1)
    noise = jnp.clip(jnp.exp(math.log(2.0) - 2.3025851 * jax.random.uniform(seeds[3], (S, U_ALL), jnp.float32) ** block_scale(seeds[3], (S, U_ALL), ((1, 4),), -0.2, 0.2)), 0.2, 2.0)
    penalty = jnp.clip(jnp.exp(math.log(4.76837158203125e-07) - 2.9957323 * jax.random.uniform(seeds[4], (AP_ALL,), jnp.float32) ** block_scale(seeds[4], (AP_ALL,), ((0, 8),), -0.2, 0.2)), 2.3841858265427618e-08, 4.76837158203125e-07)
    power = jnp.clip(jnp.exp(math.log(2.0) - 1.3862944 * jax.random.uniform(seeds[5], (AP_ALL,), jnp.float32) ** block_scale(seeds[5], (AP_ALL,), ((0, 8),), -0.2, 0.2)), 0.5, 2.0)
    return {"channel": channel, "start_precoder": start_precoder, "cluster": cluster, "noise": noise, "penalty": penalty, "power": power}


def masked_channel(channel, cluster):
    tile_users = channel.shape[-1] // cluster.shape[1]
    served = jnp.repeat(cluster, tile_users, axis=1).astype(jnp.bfloat16)
    return channel * served[None, None, :, None, :]

def stacked_rows(field):
    blocks, parts, points, antennas, users = field.shape
    return field.reshape(blocks, parts * points * antennas, users)

def partner(field):
    plain = stacked_rows(field)
    turned = stacked_rows(jnp.stack([field[:, 1], -field[:, 0]], axis=1))
    return jnp.stack([plain, turned], axis=1)

def user_terms(total, signal, noise):
    level = total + noise
    strength = signal[:, 0] * signal[:, 0] + signal[:, 1] * signal[:, 1]
    weight = level / (level - strength)
    filter_re = signal[:, 0] / level
    filter_im = signal[:, 1] / level
    coeff = weight * (filter_re * filter_re + filter_im * filter_im)
    return (weight, coeff, filter_re * weight, filter_im * weight)

def covariance(served, coeff):
    real_part = served[:, 0].astype(jnp.float32)
    imag_part = served[:, 1].astype(jnp.float32)
    first = jnp.concatenate([real_part, imag_part], axis=2)
    second = jnp.concatenate([-imag_part, real_part], axis=2)
    scaled = coeff[:, None, None, :]
    result = jnp.einsum('samk,sank->samn', first * scaled, first, precision=lax.Precision.HIGHEST)
    return result + jnp.einsum('samk,sank->samn', second * scaled, second, precision=lax.Precision.HIGHEST)

def transmit_rhs(served, scaled_re, scaled_im):
    real_part = served[:, 0].astype(jnp.float32)
    imag_part = served[:, 1].astype(jnp.float32)
    weight_re = scaled_re[:, None, None, :]
    weight_im = scaled_im[:, None, None, :]
    out_re = real_part * weight_re - imag_part * weight_im
    out_im = real_part * weight_im + imag_part * weight_re
    return jnp.concatenate([out_re, out_im], axis=2)

def cholesky_solve(system, rhs):
    factor = jnp.linalg.cholesky(system)
    middle = lax.linalg.triangular_solve(factor, rhs, left_side=True, lower=True)
    return lax.linalg.triangular_solve(factor, middle, left_side=True, lower=True, transpose_a=True)

def split_field(raw):
    antennas = raw.shape[2] // 2
    return jnp.stack([raw[:, :, :antennas], raw[:, :, antennas:]], axis=1)

def reference(channel, start_precoder, cluster, noise, penalty, power):
    served = masked_channel(channel, cluster)
    rows = stacked_rows(served).astype(jnp.float32)
    all_users = channel.shape[-1]
    antennas = channel.shape[3]
    ident = jnp.eye(2 * antennas, dtype=jnp.float32)
    precoder = start_precoder
    weight = jnp.zeros(noise.shape, jnp.float32)
    for _ in range(ITERS):
        gain = jnp.einsum('srk,scrj->sckj', rows, partner(precoder).astype(jnp.float32))
        total = lax.optimization_barrier(jnp.sum(gain * gain, axis=(1, 3)))
        signal = jnp.diagonal(gain, axis1=2, axis2=3)
        weight, coeff, scaled_re, scaled_im = user_terms(total, signal, noise)
        system = covariance(served, coeff) + penalty[None, :, None, None] * ident
        raw = cholesky_solve(system, transmit_rhs(served, scaled_re, scaled_im))
        field = split_field(raw)
        mean_sq = lax.optimization_barrier(jnp.sum(field * field, axis=(0, 1, 3, 4))) / (2.0 * field.shape[0] * antennas * all_users)
        factor = jnp.sqrt(power / (mean_sq + 1e-06))
        precoder = (field * factor[None, None, :, None, None]).astype(jnp.bfloat16)
    return (precoder, weight)
```

```python
import functools
import jax
import jax.numpy as jnp
from jax import lax
from jax.experimental import pallas as pl
from jax.experimental.pallas import tpu as pltpu
from jax.sharding import PartitionSpec as P

MESH = pl.DeviceIdType.MESH
F32 = jnp.float32
BF16 = jnp.bfloat16


def low_bit(mask):
    return mask & -mask


def three_parts(value):
    first = value.astype(BF16)
    rest = value - first.astype(F32)
    second = rest.astype(BF16)
    third = (rest - second.astype(F32)).astype(BF16)
    return first, second, third


def kernel(
    n_ap, n_ut, bits, width, chan, prec, clus, noise, penalty, power,
    out, weight_out,
    vbuf, lhs, pair, send, recv, keep, square, msgs, covs, cov_in, work, invs, raw, pows,
    v_send, v_recv, g_send, g_recv, t_send, t_recv, c_send, c_recv, i_send, i_recv, p_send, p_recv,
):
    blocks, parts, points, antennas, users = chan.shape
    rows = points * antennas
    halves = users // width
    per = covs.shape[1]
    ap = lax.axis_index("ap")
    ut = lax.axis_index("ut")

    def ap_peer(step):
        return (lax.rem(ap + step, n_ap), ut)

    def ap_flip(bit):
        return (ap + (1 << bit) - 2 * (1 << bit) * (lax.div(ap, 1 << bit) % 2), ut)

    def ut_flip_index(mask):
        index = ut
        bit = 1
        while bit <= mask:
            if mask & bit:
                index = index + bit - 2 * bit * (lax.div(ut, bit) % 2)
            bit *= 2
        return index

    def ut_flip(mask):
        return (ap, ut_flip_index(mask))

    barrier = pltpu.get_barrier_semaphore()
    for step in range(1, n_ap):
        pl.semaphore_signal(barrier, inc=1, device_id=ap_peer(step), device_id_type=MESH)
    for mask in range(1, n_ut):
        pl.semaphore_signal(barrier, inc=1, device_id=ut_flip(mask), device_id_type=MESH)
    pl.semaphore_wait(barrier, n_ap + n_ut - 2)

    pending = []

    def lanes(half):
        return pl.ds(half * width, width)

    def v_copy(mask, half):
        source = mask ^ low_bit(mask)
        if source == 0:
            src = prec.at[:, :, :, :, lanes(half)]
        else:
            src = vbuf.at[source - 1, :, :, :, :, lanes(half)]
        return pltpu.make_async_remote_copy(
            src_ref=src,
            dst_ref=vbuf.at[mask - 1, :, :, :, :, lanes(half)],
            send_sem=v_send.at[mask - 1, half],
            recv_sem=v_recv.at[mask - 1, half],
            device_id=ut_flip(low_bit(mask)),
            device_id_type=MESH,
        )

    def v_start(mask, half):
        copy = v_copy(mask, half)
        copy.start()
        pending.append(copy)

    singles = [m for m in range(n_ut - 1, 0, -1) if m == low_bit(m)]
    for half in range(halves):
        for mask in singles:
            v_start(mask, half)

    def v_arrived(mask, half):
        v_copy(mask, half).wait_recv()
        for later in range(n_ut):
            if later != low_bit(later) and (later ^ low_bit(later)) == mask:
                v_start(later, half)

    tile_users = users // clus.shape[1]
    for s in range(blocks):
        turned = []
        for part in range(parts):
            point_rows = []
            for a in range(points):
                value = chan[s, part, a].astype(F32)
                cut = [
                    value[:, c * tile_users:(c + 1) * tile_users] * clus[a, c].astype(F32)
                    for c in range(clus.shape[1])
                ]
                value = cut[0] if len(cut) == 1 else jnp.concatenate(cut, axis=1)
                point_rows.append(value)
                here = slice(part * antennas, (part + 1) * antennas)
                there = slice((1 - part) * antennas, (2 - part) * antennas)
                pair[s, a, here, 0:users] = value.astype(BF16)
                pair[s, a, there, users:2 * users] = (value if part == 0 else -value).astype(BF16)
            turned.append(jnp.concatenate(point_rows, axis=0).T)
        lhs[s, 0:users, 0:rows] = turned[0].astype(BF16)
        lhs[s, 0:users, rows:2 * rows] = turned[1].astype(BF16)
        lhs[s, users:2 * users, 0:rows] = (-turned[1]).astype(BF16)
        lhs[s, users:2 * users, rows:2 * rows] = turned[0].astype(BF16)

    all_rows = blocks * 2 * users
    own_bit = [lax.div(ap, 1 << b) % 2 for b in range(bits)]

    def g_copy(level, c):
        return pltpu.make_async_remote_copy(
            src_ref=send[level].at[c],
            dst_ref=recv[level].at[c],
            send_sem=g_send.at[level, c],
            recv_sem=g_recv.at[level, c],
            device_id=ap_flip(level),
            device_id_type=MESH,
        )

    def g_start(level, c):
        copy = g_copy(level, c)
        copy.start()
        pending.append(copy)

    some = blocks // 2

    def gains(s, slot, half):
        ref = prec if slot == 0 else vbuf.at[slot - 1]
        field = ref[s, :, :, :, half * width:(half + 1) * width].reshape(2 * rows, width)
        return jnp.dot(lhs[s], field, preferred_element_type=F32)

    def first_stage(c):
        slot, half = chunks[c]
        if slot:
            v_arrived(slot, half)
        for i in range(some):
            value = gains((1 - own_bit[0]) * some + i, slot, half)
            send[0][c, i * 2 * users:(i + 1) * 2 * users] = value.astype(BF16)
        g_start(0, c)
        for i in range(some):
            keep[0][c, i * 2 * users:(i + 1) * 2 * users] = gains(own_bit[0] * some + i, slot, half)

    def next_stage(level, c):
        g_copy(level - 1, c).wait_recv()
        if level == bits:
            total = keep[level - 1][c] + recv[level - 1][c].astype(F32)
            square[...] = total * total if c == 0 else square[...] + total * total
            return
        size = all_rows >> (level + 1)
        away = pl.ds(pl.multiple_of((1 - own_bit[level]) * size, size), size)
        mine = pl.ds(pl.multiple_of(own_bit[level] * size, size), size)
        send[level][c] = (keep[level - 1][c, away] + recv[level - 1][c, away].astype(F32)).astype(BF16)
        g_start(level, c)
        keep[level][c] = keep[level - 1][c, mine] + recv[level - 1][c, mine].astype(F32)

    chunks = [(slot, half) for slot in range(min(2, n_ut)) for half in range(halves)]
    lead = len(chunks)
    chunks += [(slot, half) for half in range(halves) for slot in range(2, n_ut)]
    count = len(chunks)
    for c in range(lead):
        first_stage(c)

    for s in range(blocks):
        sums = [jnp.zeros((1, users), F32), jnp.zeros((1, users), F32)]
        for a in range(points):
            hr = pair[s, a, 0:antennas, 0:users].astype(F32)
            hi = pair[s, a, antennas:2 * antennas, 0:users].astype(F32)
            vr = prec[s, 0, a].astype(F32)
            vi = prec[s, 1, a].astype(F32)
            sums[0] = sums[0] + jnp.sum(hr * vr + hi * vi, axis=0, keepdims=True)
            sums[1] = sums[1] + jnp.sum(hr * vi - hi * vr, axis=0, keepdims=True)
        for part in range(2):
            msgs[ap, blocks * (1 + part) + s:blocks * (1 + part) + s + 1] = sums[part]

    for i in range(count + bits - 1):
        for level in range(1, bits + 1):
            c = i - (level - 1)
            if 0 <= c < count:
                next_stage(level, c)
        if lead + i < count:
            first_stage(lead + i)

    held = all_rows >> bits
    offset = own_bit[0] * (all_rows // 2)
    for b in range(1, bits):
        offset = offset + own_bit[b] * (all_rows >> (b + 1))
    own_block = lax.div(offset, 2 * users)
    first_user = lax.rem(offset, users)
    column = jnp.sum(square[...], axis=1, keepdims=True)
    diagonal = (
        lax.broadcasted_iota(jnp.int32, (held, users), 1)
        == lax.broadcasted_iota(jnp.int32, (held, users), 0) + first_user
    )
    spread = jnp.sum(jnp.where(diagonal, column, 0.0), axis=0, keepdims=True)
    place = lax.broadcasted_iota(jnp.int32, (blocks, users), 0) == own_block
    msgs[ap, 0:blocks] = jnp.where(place, spread, 0.0)

    t_copies = [
        pltpu.make_async_remote_copy(
            src_ref=msgs.at[ap],
            dst_ref=msgs.at[ap],
            send_sem=t_send.at[step - 1],
            recv_sem=t_recv.at[step - 1],
            device_id=ap_peer(step),
            device_id_type=MESH,
        )
        for step in range(1, n_ap)
    ]
    for copy in t_copies:
        copy.start()
    for copy in t_copies:
        copy.wait_recv()
    sums = msgs[0]
    for q in range(1, n_ap):
        sums = sums + msgs[q]
    total = sums[0:blocks]
    signal_re = sums[blocks:2 * blocks]
    signal_im = sums[2 * blocks:3 * blocks]
    level = total + noise[...]
    strength = signal_re * signal_re + signal_im * signal_im
    weight = level / (level - strength)
    filter_re = signal_re / level
    filter_im = signal_im / level
    coeff = weight * (filter_re * filter_re + filter_im * filter_im)
    scaled_re = filter_re * weight
    scaled_im = filter_im * weight
    weight_out[...] = weight

    for s in range(blocks):
        for a in range(points):
            index = s * points + a
            both = pair[s, a]
            scale = coeff[s:s + 1]
            top = jnp.concatenate(
                [both[0:antennas, 0:users].astype(F32) * scale,
                 both[0:antennas, users:2 * users].astype(F32) * scale], axis=1)
            value = None
            for piece in reversed(three_parts(top)):
                term = lax.dot_general(
                    piece, both, (((1,), (1,)), ((), ())), preferred_element_type=F32)
                value = term if value is None else value + term
            covs[index // per, index % per] = value
    c_copies = [
        pltpu.make_async_remote_copy(
            src_ref=covs.at[ut_flip_index(mask)],
            dst_ref=cov_in.at[mask - 1],
            send_sem=c_send.at[mask - 1],
            recv_sem=c_recv.at[mask - 1],
            device_id=ut_flip(mask),
            device_id_type=MESH,
        )
        for mask in range(n_ut - 1, 0, -1)
    ]
    for copy in c_copies:
        copy.start()
    for copy in c_copies:
        copy.wait_recv()

    shape = (antennas, 2 * antennas)
    row_of = lax.broadcasted_iota(jnp.int32, shape, 0)
    lane_of = lax.broadcasted_iota(jnp.int32, shape, 1)
    lane_row = lane_of[0:1]
    for p in range(per):
        value = covs[ut, p]
        for mask in range(1, n_ut):
            value = value + cov_in[mask - 1, p]
        load = penalty[lax.rem(ut * per + p, points)]
        work[p] = value + jnp.where(row_of == lane_of, load, 0.0)

    sign = jnp.where(lane_row < antennas, -1.0, 1.0).astype(F32)

    def sweep(k, carry):
        is_row = row_of == k
        at_re = lane_of == k
        at_im = lane_of == k + antennas
        clear = is_row | at_re | at_im
        for p in range(per):
            value = work[p]
            row = work[p, pl.ds(k, 1)]
            pivot = jnp.sum(jnp.where(lane_row == k, row, 0.0), axis=1, keepdims=True)
            inverse = 1.0 / pivot
            col_re = jnp.sum(jnp.where(at_re, value, 0.0), axis=1, keepdims=True)
            col_im = jnp.sum(jnp.where(at_im, value, 0.0), axis=1, keepdims=True)
            row = jnp.where(lane_row == k, -inverse, jnp.where(lane_row == k + antennas, 0.0, row * inverse))
            turned = pltpu.roll(row, antennas, 1) * sign
            col_re = jnp.where(is_row, -1.0, col_re)
            col_im = jnp.where(is_row, 0.0, col_im)
            work[p] = jnp.where(clear, 0.0, value) - (col_re * row + col_im * turned)
        return carry

    lax.fori_loop(0, antennas, sweep, 0)
    for p in range(per):
        invs[ut, p] = -work[p]

    i_copies = [
        pltpu.make_async_remote_copy(
            src_ref=invs.at[ut],
            dst_ref=invs.at[ut],
            send_sem=i_send.at[mask - 1],
            recv_sem=i_recv.at[mask - 1],
            device_id=ut_flip(mask),
            device_id_type=MESH,
        )
        for mask in range(n_ut - 1, 0, -1)
    ]
    for copy in i_copies:
        copy.start()
    for copy in i_copies:
        copy.wait_recv()

    for a in range(points):
        power_row = jnp.zeros((1, users), F32)
        for s in range(blocks):
            index = s * points + a
            value = None
            for piece in reversed(three_parts(invs[index // per, index % per])):
                term = jnp.dot(piece, pair[s, a], preferred_element_type=F32)
                value = term if value is None else value + term
            base_re = value[:, 0:users]
            base_im = -value[:, users:2 * users]
            raw_re = base_re * scaled_re[s:s + 1] - base_im * scaled_im[s:s + 1]
            raw_im = base_re * scaled_im[s:s + 1] + base_im * scaled_re[s:s + 1]
            raw[s, 0, a] = raw_re
            raw[s, 1, a] = raw_im
            power_row = power_row + jnp.sum(raw_re * raw_re + raw_im * raw_im, axis=0, keepdims=True)
        pows[ut, a:a + 1] = power_row
    p_copies = [
        pltpu.make_async_remote_copy(
            src_ref=pows.at[ut],
            dst_ref=pows.at[ut],
            send_sem=p_send.at[mask - 1],
            recv_sem=p_recv.at[mask - 1],
            device_id=ut_flip(mask),
            device_id_type=MESH,
        )
        for mask in range(n_ut - 1, 0, -1)
    ]
    for copy in p_copies:
        copy.start()
    for copy in p_copies:
        copy.wait_recv()
    sums = pows[0]
    for q in range(1, n_ut):
        sums = sums + pows[q]
    mean = jnp.sum(sums, axis=1, keepdims=True) / (2.0 * blocks * antennas * users * n_ut)
    for a in range(points):
        factor = jnp.sqrt(power[a] / (mean[a:a + 1] + 1e-06))
        for s in range(blocks):
            for part in range(2):
                out[s, part, a] = (raw[s, part, a] * factor).astype(BF16)

    for copy in pending + t_copies + c_copies + i_copies + p_copies:
        copy.wait_send()


def local(n_ap, n_ut, channel, start_precoder, cluster, noise, penalty, power):
    blocks, parts, points, antennas, users = channel.shape
    bits = n_ap.bit_length() - 1
    width = 128 if users % 128 == 0 else users
    halves = users // width
    count = n_ut * halves
    rows = points * antennas
    per = blocks * points // n_ut
    all_rows = blocks * 2 * users
    sizes = [all_rows >> (b + 1) for b in range(bits)]
    vmem = pl.BlockSpec(memory_space=pltpu.VMEM)
    smem = pl.BlockSpec(memory_space=pltpu.SMEM)
    dma = pltpu.SemaphoreType.DMA
    return pl.pallas_call(
        functools.partial(kernel, n_ap, n_ut, bits, width),
        out_shape=(
            jax.ShapeDtypeStruct(channel.shape, BF16),
            jax.ShapeDtypeStruct((blocks, users), F32),
        ),
        in_specs=[vmem, vmem, smem, vmem, smem, smem],
        out_specs=(vmem, vmem),
        scratch_shapes=[
            pltpu.VMEM((n_ut - 1,) + channel.shape, BF16),
            pltpu.VMEM((blocks, 2 * users, 2 * rows), BF16),
            pltpu.VMEM((blocks, points, 2 * antennas, 2 * users), BF16),
            [pltpu.VMEM((count, size, width), BF16) for size in sizes],
            [pltpu.VMEM((count, size, width), BF16) for size in sizes],
            [pltpu.VMEM((count, size, width), F32) for size in sizes],
            pltpu.VMEM((all_rows >> bits, width), F32),
            pltpu.VMEM((n_ap, 3 * blocks, users), F32),
            pltpu.VMEM((n_ut, per, antennas, 2 * antennas), F32),
            pltpu.VMEM((n_ut - 1, per, antennas, 2 * antennas), F32),
            pltpu.VMEM((per, antennas, 2 * antennas), F32),
            pltpu.VMEM((n_ut, per, antennas, 2 * antennas), F32),
            pltpu.VMEM(channel.shape, F32),
            pltpu.VMEM((n_ut, points, users), F32),
            dma((n_ut - 1, halves)),
            dma((n_ut - 1, halves)),
            dma((bits, count)),
            dma((bits, count)),
            dma((n_ap - 1,)),
            dma((n_ap - 1,)),
            dma((n_ut - 1,)),
            dma((n_ut - 1,)),
            dma((n_ut - 1,)),
            dma((n_ut - 1,)),
            dma((n_ut - 1,)),
            dma((n_ut - 1,)),
        ],
        compiler_params=pltpu.CompilerParams(
            collective_id=0, has_side_effects=True, vmem_limit_bytes=40 * 1024 * 1024
        ),
    )(channel, start_precoder, cluster, noise, penalty, power)


def solution(mesh):
    in_specs = (
        P(None, None, "ap", None, "ut"),
        P(None, None, "ap", None, "ut"),
        P("ap", "ut"),
        P(None, "ut"),
        P("ap"),
        P("ap"),
    )
    out_specs = (P(None, None, "ap", None, "ut"), P(None, "ut"))
    body = functools.partial(local, mesh.shape["ap"], mesh.shape["ut"])
    return jax.shard_map(body, mesh=mesh, in_specs=in_specs, out_specs=out_specs, check_vma=False)
```

```python
import functools
import jax
import jax.numpy as jnp
from jax import lax
from jax.experimental import pallas as pl
from jax.experimental.pallas import tpu as pltpu
from jax.sharding import PartitionSpec as P

MESH = pl.DeviceIdType.MESH
F32 = jnp.float32
BF16 = jnp.bfloat16


def low_bit(mask):
    return mask & -mask


def three_parts(value):
    first = value.astype(BF16)
    rest = value - first.astype(F32)
    second = rest.astype(BF16)
    third = (rest - second.astype(F32)).astype(BF16)
    return first, second, third


def kernel(
    n_ap, n_ut, bits, width, chan_in, prec_in, clus, noise_in, penalty, power,
    out, weight_out,
    chan, noise, fetch, vbuf, lhs, pair, send, recv, keep, square, msgs, covs, cov_in, work, invs, raw, pows,
    v_send, v_recv, g_send, g_recv, t_send, t_recv, c_send, c_recv, i_send, i_recv, p_send, p_recv,
):
    blocks, parts, points, antennas, users = chan.shape
    rows = points * antennas
    halves = users // width
    per = covs.shape[1]
    ap = lax.axis_index("ap")
    ut = lax.axis_index("ut")

    def ap_peer(step):
        return (lax.rem(ap + step, n_ap), ut)

    def ap_flip(bit):
        return (ap + (1 << bit) - 2 * (1 << bit) * (lax.div(ap, 1 << bit) % 2), ut)

    def ut_flip_index(mask):
        index = ut
        bit = 1
        while bit <= mask:
            if mask & bit:
                index = index + bit - 2 * bit * (lax.div(ut, bit) % 2)
            bit *= 2
        return index

    def ut_flip(mask):
        return (ap, ut_flip_index(mask))

    fetches = [
        pltpu.make_async_copy(
            prec_in.at[:, :, :, :, pl.ds(half * width, width)], vbuf.at[0, half], fetch.at[half])
        for half in range(halves)
    ]
    fetches.append(pltpu.make_async_copy(chan_in, chan, fetch.at[halves]))
    fetches.append(pltpu.make_async_copy(noise_in, noise, fetch.at[halves + 1]))
    for copy in fetches:
        copy.start()

    barrier = pltpu.get_barrier_semaphore()
    for step in range(1, n_ap):
        pl.semaphore_signal(barrier, inc=1, device_id=ap_peer(step), device_id_type=MESH)
    for mask in range(1, n_ut):
        pl.semaphore_signal(barrier, inc=1, device_id=ut_flip(mask), device_id_type=MESH)
    for half in range(halves):
        fetches[half].wait()
    pl.semaphore_wait(barrier, n_ap + n_ut - 2)

    pending = []

    def v_copy(mask, half):
        return pltpu.make_async_remote_copy(
            src_ref=vbuf.at[mask ^ low_bit(mask), half],
            dst_ref=vbuf.at[mask, half],
            send_sem=v_send.at[mask - 1, half],
            recv_sem=v_recv.at[mask - 1, half],
            device_id=ut_flip(low_bit(mask)),
            device_id_type=MESH,
        )

    def v_start(mask, half):
        copy = v_copy(mask, half)
        copy.start()
        pending.append(copy)

    singles = [m for m in range(n_ut - 1, 0, -1) if m == low_bit(m)]
    for half in range(halves):
        for mask in singles:
            v_start(mask, half)

    def v_arrived(mask, half):
        v_copy(mask, half).wait_recv()
        for later in range(n_ut):
            if later != low_bit(later) and (later ^ low_bit(later)) == mask:
                v_start(later, half)

    fetches[halves].wait()
    tiles = clus.shape[0] // points
    tile_users = users // tiles
    for s in range(blocks):
        turned = []
        for part in range(parts):
            point_rows = []
            for a in range(points):
                value = chan[s, part, a].astype(F32)
                cut = [
                    value[:, c * tile_users:(c + 1) * tile_users] * clus[a * tiles + c].astype(F32)
                    for c in range(tiles)
                ]
                value = cut[0] if len(cut) == 1 else jnp.concatenate(cut, axis=1)
                point_rows.append(value)
                here = slice(part * antennas, (part + 1) * antennas)
                there = slice((1 - part) * antennas, (2 - part) * antennas)
                pair[s, a, here, 0:users] = value.astype(BF16)
                pair[s, a, there, users:2 * users] = (value if part == 0 else -value).astype(BF16)
            turned.append(jnp.concatenate(point_rows, axis=0).T)
        lhs[s, 0:users, 0:rows] = turned[0].astype(BF16)
        lhs[s, 0:users, rows:2 * rows] = turned[1].astype(BF16)
        lhs[s, users:2 * users, 0:rows] = (-turned[1]).astype(BF16)
        lhs[s, users:2 * users, rows:2 * rows] = turned[0].astype(BF16)

    all_rows = blocks * 2 * users
    own_bit = [lax.div(ap, 1 << b) % 2 for b in range(bits)]

    def order(c):
        swapped = bits > 1 and c < lead and c % 2 == 1
        return [1, 0] + list(range(2, bits)) if swapped else list(range(bits))

    def g_copy(level, c):
        return pltpu.make_async_remote_copy(
            src_ref=send[level].at[c],
            dst_ref=recv[level].at[c],
            send_sem=g_send.at[level, c],
            recv_sem=g_recv.at[level, c],
            device_id=ap_flip(order(c)[level]),
            device_id_type=MESH,
        )

    def g_start(level, c):
        copy = g_copy(level, c)
        copy.start()
        pending.append(copy)

    some = blocks // 2

    def gains(s, span, slot, half):
        field = vbuf[slot, half, s].reshape(2 * rows, width)
        return jnp.dot(lhs[s, span], field, preferred_element_type=F32)

    def half_rows(c, first, bit):
        slot, half = chunks[c]
        if first == 0:
            return [gains(bit * some + i, slice(None), slot, half) for i in range(some)]
        span = pl.ds(pl.multiple_of(bit * users, users), users)
        return [gains(s, span, slot, half) for s in range(blocks)]

    def first_stage(c):
        slot, half = chunks[c]
        if slot:
            v_arrived(slot, half)
        first = order(c)[0]
        at = 0
        for value in half_rows(c, first, 1 - own_bit[first]):
            send[0][c, at:at + value.shape[0]] = value.astype(BF16)
            at += value.shape[0]
        g_start(0, c)
        at = 0
        for value in half_rows(c, first, own_bit[first]):
            keep[0][c, at:at + value.shape[0]] = value
            at += value.shape[0]

    def next_stage(level, c):
        g_copy(level - 1, c).wait_recv()
        if level == bits:
            total = keep[level - 1][c] + recv[level - 1][c].astype(F32)
            square[...] = total * total if c == 0 else square[...] + total * total
            return
        size = all_rows >> (level + 1)
        bit = own_bit[order(c)[level]]
        away = pl.ds(pl.multiple_of((1 - bit) * size, size), size)
        mine = pl.ds(pl.multiple_of(bit * size, size), size)
        send[level][c] = (keep[level - 1][c, away] + recv[level - 1][c, away].astype(F32)).astype(BF16)
        g_start(level, c)
        keep[level][c] = keep[level - 1][c, mine] + recv[level - 1][c, mine].astype(F32)

    chunks = [(slot, half) for slot in range(min(2, n_ut)) for half in range(halves)]
    lead = len(chunks)
    chunks += [(slot, half) for half in range(halves) for slot in range(2, n_ut)]
    count = len(chunks)
    for c in range(lead):
        first_stage(c)

    for s in range(blocks):
        sums = [jnp.zeros((1, users), F32), jnp.zeros((1, users), F32)]
        for a in range(points):
            hr = pair[s, a, 0:antennas, 0:users].astype(F32)
            hi = pair[s, a, antennas:2 * antennas, 0:users].astype(F32)
            vr = jnp.concatenate([vbuf[0, h, s, 0, a] for h in range(halves)], axis=1).astype(F32)
            vi = jnp.concatenate([vbuf[0, h, s, 1, a] for h in range(halves)], axis=1).astype(F32)
            sums[0] = sums[0] + jnp.sum(hr * vr + hi * vi, axis=0, keepdims=True)
            sums[1] = sums[1] + jnp.sum(hr * vi - hi * vr, axis=0, keepdims=True)
        for part in range(2):
            msgs[ap, blocks * (1 + part) + s:blocks * (1 + part) + s + 1] = sums[part]

    for i in range(count + bits - 1):
        for level in range(1, bits + 1):
            c = i - (level - 1)
            if 0 <= c < count:
                next_stage(level, c)
        if lead + i < count:
            first_stage(lead + i)

    held = all_rows >> bits
    offset = own_bit[0] * (all_rows // 2)
    for b in range(1, bits):
        offset = offset + own_bit[b] * (all_rows >> (b + 1))
    own_block = lax.div(offset, 2 * users)
    first_user = lax.rem(offset, users)
    column = jnp.sum(square[...], axis=1, keepdims=True)
    diagonal = (
        lax.broadcasted_iota(jnp.int32, (held, users), 1)
        == lax.broadcasted_iota(jnp.int32, (held, users), 0) + first_user
    )
    spread = jnp.sum(jnp.where(diagonal, column, 0.0), axis=0, keepdims=True)
    place = lax.broadcasted_iota(jnp.int32, (blocks, users), 0) == own_block
    msgs[ap, 0:blocks] = jnp.where(place, spread, 0.0)

    t_copies = [
        pltpu.make_async_remote_copy(
            src_ref=msgs.at[ap],
            dst_ref=msgs.at[ap],
            send_sem=t_send.at[step - 1],
            recv_sem=t_recv.at[step - 1],
            device_id=ap_peer(step),
            device_id_type=MESH,
        )
        for step in range(1, n_ap)
    ]
    for copy in t_copies:
        copy.start()
    for copy in t_copies:
        copy.wait_recv()
    sums = msgs[0]
    for q in range(1, n_ap):
        sums = sums + msgs[q]
    total = sums[0:blocks]
    signal_re = sums[blocks:2 * blocks]
    signal_im = sums[2 * blocks:3 * blocks]
    fetches[halves + 1].wait()
    level = total + noise[...]
    strength = signal_re * signal_re + signal_im * signal_im
    weight = level / (level - strength)
    filter_re = signal_re / level
    filter_im = signal_im / level
    coeff = weight * (filter_re * filter_re + filter_im * filter_im)
    scaled_re = filter_re * weight
    scaled_im = filter_im * weight
    weight_out[...] = weight

    for s in range(blocks):
        for a in range(points):
            index = s * points + a
            both = pair[s, a]
            scale = coeff[s:s + 1]
            top = jnp.concatenate(
                [both[0:antennas, 0:users].astype(F32) * scale,
                 both[0:antennas, users:2 * users].astype(F32) * scale], axis=1)
            value = None
            for piece in reversed(three_parts(top)):
                term = lax.dot_general(
                    piece, both, (((1,), (1,)), ((), ())), preferred_element_type=F32)
                value = term if value is None else value + term
            covs[index // per, index % per] = value
    c_copies = [
        pltpu.make_async_remote_copy(
            src_ref=covs.at[ut_flip_index(mask)],
            dst_ref=cov_in.at[mask - 1],
            send_sem=c_send.at[mask - 1],
            recv_sem=c_recv.at[mask - 1],
            device_id=ut_flip(mask),
            device_id_type=MESH,
        )
        for mask in range(n_ut - 1, 0, -1)
    ]
    for copy in c_copies:
        copy.start()
    for copy in c_copies:
        copy.wait_recv()

    shape = (antennas, 2 * antennas)
    row_of = lax.broadcasted_iota(jnp.int32, shape, 0)
    lane_of = lax.broadcasted_iota(jnp.int32, shape, 1)
    lane_row = lane_of[0:1]
    for p in range(per):
        value = covs[ut, p]
        for mask in range(1, n_ut):
            value = value + cov_in[mask - 1, p]
        load = penalty[lax.rem(ut * per + p, points)]
        work[p] = value + jnp.where(row_of == lane_of, load, 0.0)

    sign = jnp.where(lane_row < antennas, -1.0, 1.0).astype(F32)

    def pick(row, lane):
        return jnp.sum(jnp.where(lane_of[0:row.shape[0]] == lane, row, 0.0), axis=1, keepdims=True)

    def sweep(pair_index, carry):
        k = pair_index * 2
        lane = jnp.where(lane_row >= antennas, lane_row - antennas, lane_row)
        in_pair = (lane == k) | (lane == k + 1)
        is_first = row_of == k
        is_second = row_of == k + 1
        clear = is_first | is_second | in_pair
        for p in range(per):
            value = work[p]
            row1 = work[p, pl.ds(k, 1)]
            row2 = work[p, pl.ds(k + 1, 1)]
            d1 = pick(row1, k)
            d2 = pick(row2, k + 1)
            gr = pick(row1, k + 1)
            gn = pick(row1, antennas + k + 1)
            q = 1.0 / (d1 * d2 - (gr * gr + gn * gn))
            d1, d2, gr, gn = d1 * q, d2 * q, gr * q, gn * q
            r1 = jnp.where(in_pair, jnp.where(lane_row == k, -1.0, 0.0), row1)
            r2 = jnp.where(in_pair, jnp.where(lane_row == k + 1, -1.0, 0.0), row2)
            t1 = pltpu.roll(r1, antennas, 1) * sign
            t2 = pltpu.roll(r2, antennas, 1) * sign
            p1 = d2 * r1 - (gr * r2 + gn * t2)
            tp1 = d2 * t1 - (gr * t2 - gn * r2)
            p2 = d1 * r2 - (gr * r1 - gn * t1)
            tp2 = d1 * t2 - (gr * t1 + gn * r1)
            c1r = jnp.where(is_first, -1.0, jnp.where(is_second, 0.0, pick(value, k)))
            c1n = jnp.where(is_first | is_second, 0.0, pick(value, antennas + k))
            c2r = jnp.where(is_second, -1.0, jnp.where(is_first, 0.0, pick(value, k + 1)))
            c2n = jnp.where(is_first | is_second, 0.0, pick(value, antennas + k + 1))
            work[p] = jnp.where(clear, 0.0, value) - ((c1r * p1 + c1n * tp1) + (c2r * p2 + c2n * tp2))
        return carry

    lax.fori_loop(0, antennas // 2, sweep, 0)
    for p in range(per):
        invs[ut, p] = -work[p]

    i_copies = [
        pltpu.make_async_remote_copy(
            src_ref=invs.at[ut],
            dst_ref=invs.at[ut],
            send_sem=i_send.at[mask - 1],
            recv_sem=i_recv.at[mask - 1],
            device_id=ut_flip(mask),
            device_id_type=MESH,
        )
        for mask in range(n_ut - 1, 0, -1)
    ]
    for copy in i_copies:
        copy.start()
    for copy in i_copies:
        copy.wait_recv()

    for a in range(points):
        power_row = jnp.zeros((1, users), F32)
        for s in range(blocks):
            index = s * points + a
            value = None
            for piece in reversed(three_parts(invs[index // per, index % per])):
                term = jnp.dot(piece, pair[s, a], preferred_element_type=F32)
                value = term if value is None else value + term
            base_re = value[:, 0:users]
            base_im = -value[:, users:2 * users]
            raw_re = base_re * scaled_re[s:s + 1] - base_im * scaled_im[s:s + 1]
            raw_im = base_re * scaled_im[s:s + 1] + base_im * scaled_re[s:s + 1]
            raw[s, 0, a] = raw_re
            raw[s, 1, a] = raw_im
            power_row = power_row + jnp.sum(raw_re * raw_re + raw_im * raw_im, axis=0, keepdims=True)
        pows[ut, a:a + 1] = power_row
    p_copies = [
        pltpu.make_async_remote_copy(
            src_ref=pows.at[ut],
            dst_ref=pows.at[ut],
            send_sem=p_send.at[mask - 1],
            recv_sem=p_recv.at[mask - 1],
            device_id=ut_flip(mask),
            device_id_type=MESH,
        )
        for mask in range(n_ut - 1, 0, -1)
    ]
    for copy in p_copies:
        copy.start()
    for copy in p_copies:
        copy.wait_recv()
    sums = pows[0]
    for q in range(1, n_ut):
        sums = sums + pows[q]
    mean = jnp.sum(sums, axis=1, keepdims=True) / (2.0 * blocks * antennas * users * n_ut)
    for a in range(points):
        factor = jnp.sqrt(power[a] / (mean[a:a + 1] + 1e-06))
        for s in range(blocks):
            for part in range(2):
                out[s, part, a] = (raw[s, part, a] * factor).astype(BF16)

    for copy in pending + t_copies + c_copies + i_copies + p_copies:
        copy.wait_send()


def local(n_ap, n_ut, channel, start_precoder, cluster, noise, penalty, power):
    blocks, parts, points, antennas, users = channel.shape
    bits = n_ap.bit_length() - 1
    width = 128 if users % 128 == 0 else users
    halves = users // width
    count = n_ut * halves
    rows = points * antennas
    per = blocks * points // n_ut
    all_rows = blocks * 2 * users
    sizes = [all_rows >> (b + 1) for b in range(bits)]
    vmem = pl.BlockSpec(memory_space=pltpu.VMEM)
    smem = pl.BlockSpec(memory_space=pltpu.SMEM)
    hbm = pl.BlockSpec(memory_space=pl.ANY)
    dma = pltpu.SemaphoreType.DMA
    return pl.pallas_call(
        functools.partial(kernel, n_ap, n_ut, bits, width),
        out_shape=(
            jax.ShapeDtypeStruct(channel.shape, BF16),
            jax.ShapeDtypeStruct((blocks, users), F32),
        ),
        in_specs=[hbm, hbm, smem, hbm, smem, smem],
        out_specs=(vmem, vmem),
        scratch_shapes=[
            pltpu.VMEM(channel.shape, BF16),
            pltpu.VMEM(noise.shape, F32),
            dma((halves + 2,)),
            pltpu.VMEM((n_ut, halves) + channel.shape[:-1] + (width,), BF16),
            pltpu.VMEM((blocks, 2 * users, 2 * rows), BF16),
            pltpu.VMEM((blocks, points, 2 * antennas, 2 * users), BF16),
            [pltpu.VMEM((count, size, width), BF16) for size in sizes],
            [pltpu.VMEM((count, size, width), BF16) for size in sizes],
            [pltpu.VMEM((count, size, width), F32) for size in sizes],
            pltpu.VMEM((all_rows >> bits, width), F32),
            pltpu.VMEM((n_ap, 3 * blocks, users), F32),
            pltpu.VMEM((n_ut, per, antennas, 2 * antennas), F32),
            pltpu.VMEM((n_ut - 1, per, antennas, 2 * antennas), F32),
            pltpu.VMEM((per, antennas, 2 * antennas), F32),
            pltpu.VMEM((n_ut, per, antennas, 2 * antennas), F32),
            pltpu.VMEM(channel.shape, F32),
            pltpu.VMEM((n_ut, points, users), F32),
            dma((n_ut - 1, halves)),
            dma((n_ut - 1, halves)),
            dma((bits, count)),
            dma((bits, count)),
            dma((n_ap - 1,)),
            dma((n_ap - 1,)),
            dma((n_ut - 1,)),
            dma((n_ut - 1,)),
            dma((n_ut - 1,)),
            dma((n_ut - 1,)),
            dma((n_ut - 1,)),
            dma((n_ut - 1,)),
        ],
        compiler_params=pltpu.CompilerParams(
            collective_id=0, has_side_effects=True, vmem_limit_bytes=56 * 1024 * 1024
        ),
    )(channel, start_precoder, cluster.reshape(-1), noise, penalty, power)


def solution(mesh):
    in_specs = (
        P(None, None, "ap", None, "ut"),
        P(None, None, "ap", None, "ut"),
        P("ap", "ut"),
        P(None, "ut"),
        P("ap"),
        P("ap"),
    )
    out_specs = (P(None, None, "ap", None, "ut"), P(None, "ut"))
    body = functools.partial(local, mesh.shape["ap"], mesh.shape["ut"])
    return jax.shard_map(body, mesh=mesh, in_specs=in_specs, out_specs=out_specs, check_vma=False)
```

```python
import functools
import jax
import jax.numpy as jnp
from jax import lax
from jax.experimental import pallas as pl
from jax.experimental.pallas import tpu as pltpu
from jax.sharding import PartitionSpec as P

MESH = pl.DeviceIdType.MESH
F32 = jnp.float32
BF16 = jnp.bfloat16


def low_bit(mask):
    return mask & -mask


def three_parts(value):
    first = value.astype(BF16)
    rest = value - first.astype(F32)
    second = rest.astype(BF16)
    third = (rest - second.astype(F32)).astype(BF16)
    return first, second, third


def kernel(
    n_ap, n_ut, bits, width, chan_in, prec_in, clus, noise_in, penalty, power,
    out, weight_out,
    chan, noise, fetch, vbuf, lhs, pair, send, recv, keep, square, msgs, covs, cov_in, work, invs, raw, pows,
    v_send, v_recv, g_send, g_recv, t_send, t_recv, c_send, c_recv, i_send, i_recv, p_send, p_recv,
):
    blocks, parts, points, antennas, users = chan.shape
    rows = points * antennas
    halves = users // width
    per = covs.shape[1]
    ap = lax.axis_index("ap")
    ut = lax.axis_index("ut")

    def ap_peer(step):
        return (lax.rem(ap + step, n_ap), ut)

    def ap_flip(bit):
        return (ap + (1 << bit) - 2 * (1 << bit) * (lax.div(ap, 1 << bit) % 2), ut)

    def ut_flip_index(mask):
        index = ut
        bit = 1
        while bit <= mask:
            if mask & bit:
                index = index + bit - 2 * bit * (lax.div(ut, bit) % 2)
            bit *= 2
        return index

    def ut_flip(mask):
        return (ap, ut_flip_index(mask))

    fetches = [
        pltpu.make_async_copy(
            prec_in.at[:, :, :, :, pl.ds(half * width, width)], vbuf.at[0, half], fetch.at[half])
        for half in range(halves)
    ]
    fetches.append(pltpu.make_async_copy(chan_in, chan, fetch.at[halves]))
    fetches.append(pltpu.make_async_copy(noise_in, noise, fetch.at[halves + 1]))
    for copy in fetches:
        copy.start()

    barrier = pltpu.get_barrier_semaphore()
    for step in range(1, n_ap):
        pl.semaphore_signal(barrier, inc=1, device_id=ap_peer(step), device_id_type=MESH)
    for mask in range(1, n_ut):
        pl.semaphore_signal(barrier, inc=1, device_id=ut_flip(mask), device_id_type=MESH)
    for half in range(halves):
        fetches[half].wait()
    pl.semaphore_wait(barrier, n_ap + n_ut - 2)

    pending = []

    def v_copy(mask, half):
        return pltpu.make_async_remote_copy(
            src_ref=vbuf.at[mask ^ low_bit(mask), half],
            dst_ref=vbuf.at[mask, half],
            send_sem=v_send.at[mask - 1, half],
            recv_sem=v_recv.at[mask - 1, half],
            device_id=ut_flip(low_bit(mask)),
            device_id_type=MESH,
        )

    def v_start(mask, half):
        copy = v_copy(mask, half)
        copy.start()
        pending.append(copy)

    singles = [m for m in range(n_ut - 1, 0, -1) if m == low_bit(m)]
    for half in range(halves):
        for mask in singles:
            v_start(mask, half)

    def v_arrived(mask, half):
        v_copy(mask, half).wait_recv()
        for later in range(n_ut):
            if later != low_bit(later) and (later ^ low_bit(later)) == mask:
                v_start(later, half)

    fetches[halves].wait()
    tiles = clus.shape[0] // points
    tile_users = users // tiles
    for s in range(blocks):
        turned = []
        for part in range(parts):
            point_rows = []
            for a in range(points):
                value = chan[s, part, a].astype(F32)
                cut = [
                    value[:, c * tile_users:(c + 1) * tile_users] * clus[a * tiles + c].astype(F32)
                    for c in range(tiles)
                ]
                value = cut[0] if len(cut) == 1 else jnp.concatenate(cut, axis=1)
                point_rows.append(value)
                here = slice(part * antennas, (part + 1) * antennas)
                there = slice((1 - part) * antennas, (2 - part) * antennas)
                pair[s, a, here, 0:users] = value.astype(BF16)
                pair[s, a, there, users:2 * users] = (value if part == 0 else -value).astype(BF16)
            turned.append(jnp.concatenate(point_rows, axis=0).T)
        lhs[s, 0:users, 0:rows] = turned[0].astype(BF16)
        lhs[s, 0:users, rows:2 * rows] = turned[1].astype(BF16)
        lhs[s, users:2 * users, 0:rows] = (-turned[1]).astype(BF16)
        lhs[s, users:2 * users, rows:2 * rows] = turned[0].astype(BF16)

    all_rows = blocks * 2 * users
    own_bit = [lax.div(ap, 1 << b) % 2 for b in range(bits)]

    def order(c):
        swapped = bits > 1 and c >= lead and (c - lead) % 2 == 1
        return [1, 0] + list(range(2, bits)) if swapped else list(range(bits))

    def g_copy(level, c):
        return pltpu.make_async_remote_copy(
            src_ref=send[level].at[c],
            dst_ref=recv[level].at[c],
            send_sem=g_send.at[level, c],
            recv_sem=g_recv.at[level, c],
            device_id=ap_flip(order(c)[level]),
            device_id_type=MESH,
        )

    def g_start(level, c):
        copy = g_copy(level, c)
        copy.start()
        pending.append(copy)

    some = blocks // 2

    def gains(s, span, slot, half):
        field = vbuf[slot, half, s].reshape(2 * rows, width)
        return jnp.dot(lhs[s, span], field, preferred_element_type=F32)

    def half_rows(c, first, bit):
        slot, half = chunks[c]
        if first == 0:
            return [gains(bit * some + i, slice(None), slot, half) for i in range(some)]
        span = pl.ds(pl.multiple_of(bit * users, users), users)
        return [gains(s, span, slot, half) for s in range(blocks)]

    def first_stage(c):
        slot, half = chunks[c]
        if slot:
            v_arrived(slot, half)
        first = order(c)[0]
        at = 0
        for value in half_rows(c, first, 1 - own_bit[first]):
            send[0][c, at:at + value.shape[0]] = value.astype(BF16)
            at += value.shape[0]
        g_start(0, c)
        at = 0
        for value in half_rows(c, first, own_bit[first]):
            keep[0][c, at:at + value.shape[0]] = value
            at += value.shape[0]

    def next_stage(level, c):
        g_copy(level - 1, c).wait_recv()
        if level == bits:
            total = keep[level - 1][c] + recv[level - 1][c].astype(F32)
            square[...] = total * total if c == 0 else square[...] + total * total
            return
        size = all_rows >> (level + 1)
        bit = own_bit[order(c)[level]]
        away = pl.ds(pl.multiple_of((1 - bit) * size, size), size)
        mine = pl.ds(pl.multiple_of(bit * size, size), size)
        send[level][c] = (keep[level - 1][c, away] + recv[level - 1][c, away].astype(F32)).astype(BF16)
        g_start(level, c)
        keep[level][c] = keep[level - 1][c, mine] + recv[level - 1][c, mine].astype(F32)

    chunks = [(slot, half) for slot in range(min(2, n_ut)) for half in range(halves)]
    lead = len(chunks)
    chunks += [(slot, half) for half in range(halves) for slot in range(2, n_ut)]
    count = len(chunks)
    for c in range(lead):
        first_stage(c)

    for s in range(blocks):
        sums = [jnp.zeros((1, users), F32), jnp.zeros((1, users), F32)]
        for a in range(points):
            hr = pair[s, a, 0:antennas, 0:users].astype(F32)
            hi = pair[s, a, antennas:2 * antennas, 0:users].astype(F32)
            vr = jnp.concatenate([vbuf[0, h, s, 0, a] for h in range(halves)], axis=1).astype(F32)
            vi = jnp.concatenate([vbuf[0, h, s, 1, a] for h in range(halves)], axis=1).astype(F32)
            sums[0] = sums[0] + jnp.sum(hr * vr + hi * vi, axis=0, keepdims=True)
            sums[1] = sums[1] + jnp.sum(hr * vi - hi * vr, axis=0, keepdims=True)
        for part in range(2):
            msgs[ap, blocks * (1 + part) + s:blocks * (1 + part) + s + 1] = sums[part]

    turn = sorted(range(count), key=lambda c: c if c < lead or (c - lead) % 2 == 0 else c - 1.5)
    for i in range(count + bits - 1):
        for level in range(1, bits + 1):
            at = i - (level - 1)
            if 0 <= at < count:
                next_stage(level, turn[at])
        if lead + i < count:
            first_stage(lead + i)

    held = all_rows >> bits
    offset = own_bit[0] * (all_rows // 2)
    for b in range(1, bits):
        offset = offset + own_bit[b] * (all_rows >> (b + 1))
    own_block = lax.div(offset, 2 * users)
    first_user = lax.rem(offset, users)
    column = jnp.sum(square[...], axis=1, keepdims=True)
    diagonal = (
        lax.broadcasted_iota(jnp.int32, (held, users), 1)
        == lax.broadcasted_iota(jnp.int32, (held, users), 0) + first_user
    )
    spread = jnp.sum(jnp.where(diagonal, column, 0.0), axis=0, keepdims=True)
    place = lax.broadcasted_iota(jnp.int32, (blocks, users), 0) == own_block
    msgs[ap, 0:blocks] = jnp.where(place, spread, 0.0)

    t_copies = [
        pltpu.make_async_remote_copy(
            src_ref=msgs.at[ap],
            dst_ref=msgs.at[ap],
            send_sem=t_send.at[step - 1],
            recv_sem=t_recv.at[step - 1],
            device_id=ap_peer(step),
            device_id_type=MESH,
        )
        for step in range(1, n_ap)
    ]
    for copy in t_copies:
        copy.start()
    for copy in t_copies:
        copy.wait_recv()
    sums = msgs[0]
    for q in range(1, n_ap):
        sums = sums + msgs[q]
    total = sums[0:blocks]
    signal_re = sums[blocks:2 * blocks]
    signal_im = sums[2 * blocks:3 * blocks]
    fetches[halves + 1].wait()
    level = total + noise[...]
    strength = signal_re * signal_re + signal_im * signal_im
    weight = level / (level - strength)
    filter_re = signal_re / level
    filter_im = signal_im / level
    coeff = weight * (filter_re * filter_re + filter_im * filter_im)
    scaled_re = filter_re * weight
    scaled_im = filter_im * weight
    weight_out[...] = weight

    for s in range(blocks):
        for a in range(points):
            index = s * points + a
            both = pair[s, a]
            scale = coeff[s:s + 1]
            top = jnp.concatenate(
                [both[0:antennas, 0:users].astype(F32) * scale,
                 both[0:antennas, users:2 * users].astype(F32) * scale], axis=1)
            value = None
            for piece in reversed(three_parts(top)):
                term = lax.dot_general(
                    piece, both, (((1,), (1,)), ((), ())), preferred_element_type=F32)
                value = term if value is None else value + term
            covs[index // per, index % per] = value
    c_copies = [
        pltpu.make_async_remote_copy(
            src_ref=covs.at[ut_flip_index(mask)],
            dst_ref=cov_in.at[mask - 1],
            send_sem=c_send.at[mask - 1],
            recv_sem=c_recv.at[mask - 1],
            device_id=ut_flip(mask),
            device_id_type=MESH,
        )
        for mask in range(n_ut - 1, 0, -1)
    ]
    for copy in c_copies:
        copy.start()
    for copy in c_copies:
        copy.wait_recv()

    shape = (antennas, 2 * antennas)
    row_of = lax.broadcasted_iota(jnp.int32, shape, 0)
    lane_of = lax.broadcasted_iota(jnp.int32, shape, 1)
    lane_row = lane_of[0:1]
    for p in range(per):
        value = covs[ut, p]
        for mask in range(1, n_ut):
            value = value + cov_in[mask - 1, p]
        load = penalty[lax.rem(ut * per + p, points)]
        work[p] = value + jnp.where(row_of == lane_of, load, 0.0)

    sign = jnp.where(lane_row < antennas, -1.0, 1.0).astype(F32)

    def pick(row, lane):
        return jnp.sum(jnp.where(lane_of[0:row.shape[0]] == lane, row, 0.0), axis=1, keepdims=True)

    def sweep(pair_index, carry):
        k = pair_index * 2
        lane = jnp.where(lane_row >= antennas, lane_row - antennas, lane_row)
        in_pair = (lane == k) | (lane == k + 1)
        is_first = row_of == k
        is_second = row_of == k + 1
        clear = is_first | is_second | in_pair
        for p in range(per):
            value = work[p]
            row1 = work[p, pl.ds(k, 1)]
            row2 = work[p, pl.ds(k + 1, 1)]
            d1 = pick(row1, k)
            d2 = pick(row2, k + 1)
            gr = pick(row1, k + 1)
            gn = pick(row1, antennas + k + 1)
            q = 1.0 / (d1 * d2 - (gr * gr + gn * gn))
            d1, d2, gr, gn = d1 * q, d2 * q, gr * q, gn * q
            r1 = jnp.where(in_pair, jnp.where(lane_row == k, -1.0, 0.0), row1)
            r2 = jnp.where(in_pair, jnp.where(lane_row == k + 1, -1.0, 0.0), row2)
            t1 = pltpu.roll(r1, antennas, 1) * sign
            t2 = pltpu.roll(r2, antennas, 1) * sign
            p1 = d2 * r1 - (gr * r2 + gn * t2)
            tp1 = d2 * t1 - (gr * t2 - gn * r2)
            p2 = d1 * r2 - (gr * r1 - gn * t1)
            tp2 = d1 * t2 - (gr * t1 + gn * r1)
            c1r = jnp.where(is_first, -1.0, jnp.where(is_second, 0.0, pick(value, k)))
            c1n = jnp.where(is_first | is_second, 0.0, pick(value, antennas + k))
            c2r = jnp.where(is_second, -1.0, jnp.where(is_first, 0.0, pick(value, k + 1)))
            c2n = jnp.where(is_first | is_second, 0.0, pick(value, antennas + k + 1))
            work[p] = jnp.where(clear, 0.0, value) - ((c1r * p1 + c1n * tp1) + (c2r * p2 + c2n * tp2))
        return carry

    lax.fori_loop(0, antennas // 2, sweep, 0, unroll=2)
    for p in range(per):
        invs[ut, p] = -work[p]

    i_copies = [
        pltpu.make_async_remote_copy(
            src_ref=invs.at[ut],
            dst_ref=invs.at[ut],
            send_sem=i_send.at[mask - 1],
            recv_sem=i_recv.at[mask - 1],
            device_id=ut_flip(mask),
            device_id_type=MESH,
        )
        for mask in range(n_ut - 1, 0, -1)
    ]
    for copy in i_copies:
        copy.start()
    for copy in i_copies:
        copy.wait_recv()

    for a in range(points):
        power_row = jnp.zeros((1, users), F32)
        for s in range(blocks):
            index = s * points + a
            value = None
            for piece in reversed(three_parts(invs[index // per, index % per])):
                term = jnp.dot(piece, pair[s, a], preferred_element_type=F32)
                value = term if value is None else value + term
            base_re = value[:, 0:users]
            base_im = -value[:, users:2 * users]
            raw_re = base_re * scaled_re[s:s + 1] - base_im * scaled_im[s:s + 1]
            raw_im = base_re * scaled_im[s:s + 1] + base_im * scaled_re[s:s + 1]
            raw[s, 0, a] = raw_re
            raw[s, 1, a] = raw_im
            power_row = power_row + jnp.sum(raw_re * raw_re + raw_im * raw_im, axis=0, keepdims=True)
        pows[ut, a:a + 1] = power_row
    p_copies = [
        pltpu.make_async_remote_copy(
            src_ref=pows.at[ut],
            dst_ref=pows.at[ut],
            send_sem=p_send.at[mask - 1],
            recv_sem=p_recv.at[mask - 1],
            device_id=ut_flip(mask),
            device_id_type=MESH,
        )
        for mask in range(n_ut - 1, 0, -1)
    ]
    for copy in p_copies:
        copy.start()
    for copy in p_copies:
        copy.wait_recv()
    sums = pows[0]
    for q in range(1, n_ut):
        sums = sums + pows[q]
    mean = jnp.sum(sums, axis=1, keepdims=True) / (2.0 * blocks * antennas * users * n_ut)
    for a in range(points):
        factor = jnp.sqrt(power[a] / (mean[a:a + 1] + 1e-06))
        for s in range(blocks):
            for part in range(2):
                out[s, part, a] = (raw[s, part, a] * factor).astype(BF16)

    for copy in pending + t_copies + c_copies + i_copies + p_copies:
        copy.wait_send()


def local(n_ap, n_ut, channel, start_precoder, cluster, noise, penalty, power):
    blocks, parts, points, antennas, users = channel.shape
    bits = n_ap.bit_length() - 1
    width = 128 if users % 128 == 0 else users
    halves = users // width
    count = n_ut * halves
    rows = points * antennas
    per = blocks * points // n_ut
    all_rows = blocks * 2 * users
    sizes = [all_rows >> (b + 1) for b in range(bits)]
    vmem = pl.BlockSpec(memory_space=pltpu.VMEM)
    smem = pl.BlockSpec(memory_space=pltpu.SMEM)
    hbm = pl.BlockSpec(memory_space=pl.ANY)
    dma = pltpu.SemaphoreType.DMA
    return pl.pallas_call(
        functools.partial(kernel, n_ap, n_ut, bits, width),
        out_shape=(
            jax.ShapeDtypeStruct(channel.shape, BF16),
            jax.ShapeDtypeStruct((blocks, users), F32),
        ),
        in_specs=[hbm, hbm, smem, hbm, smem, smem],
        out_specs=(vmem, vmem),
        scratch_shapes=[
            pltpu.VMEM(channel.shape, BF16),
            pltpu.VMEM(noise.shape, F32),
            dma((halves + 2,)),
            pltpu.VMEM((n_ut, halves) + channel.shape[:-1] + (width,), BF16),
            pltpu.VMEM((blocks, 2 * users, 2 * rows), BF16),
            pltpu.VMEM((blocks, points, 2 * antennas, 2 * users), BF16),
            [pltpu.VMEM((count, size, width), BF16) for size in sizes],
            [pltpu.VMEM((count, size, width), BF16) for size in sizes],
            [pltpu.VMEM((count, size, width), F32) for size in sizes],
            pltpu.VMEM((all_rows >> bits, width), F32),
            pltpu.VMEM((n_ap, 3 * blocks, users), F32),
            pltpu.VMEM((n_ut, per, antennas, 2 * antennas), F32),
            pltpu.VMEM((n_ut - 1, per, antennas, 2 * antennas), F32),
            pltpu.VMEM((per, antennas, 2 * antennas), F32),
            pltpu.VMEM((n_ut, per, antennas, 2 * antennas), F32),
            pltpu.VMEM(channel.shape, F32),
            pltpu.VMEM((n_ut, points, users), F32),
            dma((n_ut - 1, halves)),
            dma((n_ut - 1, halves)),
            dma((bits, count)),
            dma((bits, count)),
            dma((n_ap - 1,)),
            dma((n_ap - 1,)),
            dma((n_ut - 1,)),
            dma((n_ut - 1,)),
            dma((n_ut - 1,)),
            dma((n_ut - 1,)),
            dma((n_ut - 1,)),
            dma((n_ut - 1,)),
        ],
        compiler_params=pltpu.CompilerParams(
            collective_id=0, has_side_effects=True, vmem_limit_bytes=56 * 1024 * 1024
        ),
    )(channel, start_precoder, cluster.reshape(-1), noise, penalty, power)


def solution(mesh):
    in_specs = (
        P(None, None, "ap", None, "ut"),
        P(None, None, "ap", None, "ut"),
        P("ap", "ut"),
        P(None, "ut"),
        P("ap"),
        P("ap"),
    )
    out_specs = (P(None, None, "ap", None, "ut"), P(None, "ut"))
    body = functools.partial(local, mesh.shape["ap"], mesh.shape["ut"])
    return jax.shard_map(body, mesh=mesh, in_specs=in_specs, out_specs=out_specs, check_vma=False)
```
